512 devices in a mesh: dp: 64 (over z_lo, x, core), tp: 8 (over z_hi, y).
Axes of the slice: x: 4, y: 4, z: 16 (z_hi: 2, z_lo: 8; z = z_hi * 8 + z_lo), core: 2. Of those that a mesh axis runs over, the one named last changes fastest.
Arguments:
- attention: bfloat16 [39424, 4096], P('dp', 'tp'), may hold values from -6 to 6
- residual: bfloat16 [39424, 4096], P('dp', 'tp'), may hold values from -6 to 6
- out_weight: bfloat16 [4096, 4096], P('dp', 'tp'), may hold values from -0.09375 to 0.09375
- norm_gain: float32 [4096], P('tp'), may hold values from 0.5 to 1.5
- lengths: int32 [512], P('dp'), may hold values from 8 to 77
- adapter: bfloat16 [4096, 1280], P('tp', 'dp'), may hold values from -0.09375 to 0.09375
- images: float32 [512, 1280], P('dp'), may hold values from -6 to 6
- log_scale: float32 [1], replicated, may hold values from 2 to 3
- logit_bias: float32 [1], replicated, may hold values from -2 to 0
Outputs:
- mean_loss: float32 [1], replicated
- pooled_grad: float32 [512, 4096], P('dp', 'tp')
- image_grad: float32 [512, 1280], P('dp')
The draws below stay inside these ranges and needn't reach their ends.
All inputs are finite; a program needn't handle non-finite values.
Results may differ from the reference program's by a relative error of at most 0.00075.
The reference program's roundings to bfloat16 on the way (of `pooled`) count: a program that leaves them out, or rounds other values in their place, can miss the bound.
Values may be sent and summed in bfloat16 or wider, within the bound.
No kernel may reach another device: no remote copies, remote signals or barrier semaphores. Data moves between devices by JAX's collectives and lax.ppermute only.
A program may use at most 64 MiB of HBM per device.

```python
import jax
import jax.numpy as jnp
from jax import lax

D = 4096
E = 1280
SEQ = 77
CAP_DEV = 8
CAPTIONS = 512
TOKENS = 39424
N_DP = 64


def set_ends(array, key, least, high):
    longest = array.shape.index(max(array.shape))
    spots = []
    for shift in (0, 1):
        where = [jax.random.randint(jax.random.fold_in(key, axis), (), 0, length) for axis, length in enumerate(array.shape)]
        where[longest] = (where[longest] + shift) % array.shape[longest]
        spots.append(tuple(where))
    return array.at[spots[0]].set(least).at[spots[1]].set(high)


def steps_of(key, shape, shards, low, top_value):
    factor_of = 1.0
    for dim, parts in shards:
        draws = jax.random.uniform(jax.random.fold_in(jax.random.fold_in(key, 6), dim), (parts,), jnp.float32, low / len(shards), top_value / len(shards))
        factor_of = factor_of * jnp.repeat(jnp.exp(draws), shape[dim] // parts).reshape((-1,) + (1,) * (len(shape) - 1 - dim))
    return factor_of


def normal_values(rng, shape, width, reach, split=(), kind=jnp.bfloat16):
    values = jax.random.normal(rng, shape, jnp.float32) * width
    if len(split) > 0:
        values = steps_of(rng, shape, split, -0.22, 0.18) * values
    return jnp.clip(values, min=-reach, max=reach).astype(kind)


def setup_inputs(seed: int = 0) -> dict:
    splits = jax.random.split(jax.random.key(seed), 10)
    attention = normal_values(splits[0], (TOKENS, D), 1.0, 6.0, ((0, 64), (1, 8)))
    residual = normal_values(splits[1], (TOKENS, D), 1.0, 6.0, ((0, 64), (1, 8)))
    out_weight = normal_values(splits[2], (D, D), D ** -0.5, 0.09375, ((0, 64), (1, 8)))
    norm_gain = jnp.clip(1.0 + 0.1 * jax.random.normal(splits[3], (D,), jnp.float32), 0.5, 1.5)
    lengths = set_ends(jax.random.randint(splits[4], (CAPTIONS,), 8, SEQ + 1), jax.random.fold_in(splits[4], 1), 8, SEQ).astype(jnp.int32)
    adapter = normal_values(splits[5], (D, E), D ** -0.5, 0.09375, ((0, 8), (1, 64)))
    images = normal_values(splits[6], (CAPTIONS, E), 1.0, 6.0, ((0, 64),), jnp.float32)
    log_scale = jnp.clip(jax.random.uniform(splits[7], (1,), jnp.float32, 2.0, 3.0), 2.0, 3.0)
    logit_bias = jnp.clip(jax.random.uniform(splits[8], (1,), jnp.float32, -2.0, 0.0), -2.0, 0.0)
    return {"attention": attention, "residual": residual, "out_weight": out_weight, "norm_gain": norm_gain, "lengths": lengths, "adapter": adapter, "images": images, "log_scale": log_scale, "logit_bias": logit_bias}


def reference(attention, residual, out_weight, norm_gain, lengths, adapter, images, log_scale, logit_bias):
    attn_blocks = attention.reshape(N_DP, CAP_DEV * SEQ, D)
    resid_blocks = residual.reshape(N_DP, CAP_DEV * SEQ, D)
    length_blocks = lengths.reshape(N_DP, CAP_DEV)

    def pool_block(block_args):
        attn_rows, resid_rows, len_rows = block_args
        hidden = resid_rows.astype(jnp.float32) + jnp.dot(attn_rows, out_weight, preferred_element_type=jnp.float32)
        mean_square = lax.optimization_barrier(jnp.mean(hidden * hidden, axis=1, keepdims=True))
        normed = hidden * lax.rsqrt(mean_square + 1e-05) * norm_gain[None, :]
        normed = normed.reshape(CAP_DEV, SEQ, D)
        positions = jnp.arange(SEQ, dtype=jnp.int32)
        live_mask = (positions[None, :] < len_rows[:, None]).astype(jnp.float32)
        summed = lax.optimization_barrier(jnp.sum(normed * live_mask[:, :, None], axis=1))
        return (summed / len_rows.astype(jnp.float32)[:, None]).astype(jnp.bfloat16)
    pooled = lax.map(pool_block, (attn_blocks, resid_blocks, length_blocks)).reshape(CAPTIONS, D)
    raw_text = jnp.dot(pooled, adapter, preferred_element_type=jnp.float32)
    text_norm = jnp.sqrt(lax.optimization_barrier(jnp.sum(raw_text * raw_text, axis=1, keepdims=True)) + 1e-06)
    text_unit = raw_text / text_norm
    image_norm = jnp.sqrt(lax.optimization_barrier(jnp.sum(images * images, axis=1, keepdims=True)) + 1e-06)
    picture = images / image_norm
    logit_scale = jnp.exp(log_scale[0])
    logits = logit_scale * jnp.dot(text_unit, picture.T, precision=lax.Precision.HIGHEST) + logit_bias[0]
    labels = jnp.eye(CAPTIONS, dtype=jnp.float32)
    pair_total = -jnp.sum(jax.nn.log_sigmoid((2.0 * labels - 1.0) * logits))
    mean_loss = (pair_total / (CAPTIONS * CAPTIONS)).reshape(1)
    pair_slope = jax.nn.sigmoid(logits) - labels
    text_grad = logit_scale * jnp.dot(pair_slope, picture, precision=lax.Precision.HIGHEST)
    picture_grad = logit_scale * jnp.dot(pair_slope.T, text_unit, precision=lax.Precision.HIGHEST)
    raw_grad = (text_grad - text_unit * lax.optimization_barrier(jnp.sum(text_unit * text_grad, axis=1, keepdims=True))) / text_norm
    pooled_grad = jnp.dot(raw_grad, adapter.astype(jnp.float32).T, precision=lax.Precision.HIGHEST)
    image_grad = (picture_grad - picture * lax.optimization_barrier(jnp.sum(picture * picture_grad, axis=1, keepdims=True))) / image_norm
    return (mean_loss, pooled_grad, image_grad)
```

```python
import jax
import jax.numpy as jnp
from jax import lax
from jax.sharding import Mesh, PartitionSpec as P

F32 = jnp.float32
BF16 = jnp.bfloat16
F16 = jnp.float16
SIZES = {"zl": 8, "x": 4, "c": 2, "zh": 2, "y": 4}
TP = ("zh", "y")


def swap(v, axis):
    return lax.ppermute(v, axis, [(0, 1), (1, 0)])


def shift(v, axis, by):
    n = SIZES[axis]
    return lax.ppermute(v, axis, [(i, (i + by) % n) for i in range(n)])


def around_y(v):
    return [v] + [shift(v, "y", s) for s in (1, 2, 3)]


def add_products(total, blocks, weights, y):
    for back, block in enumerate(blocks):
        w = lax.dynamic_index_in_dim(weights, (y - back) % 4, 0, keepdims=False)
        total = total + jnp.dot(block, w, preferred_element_type=F32)
    return total


def gather(v, axes):
    n = 1
    for a in axes:
        n *= SIZES[a]
    return lax.all_to_all(jnp.broadcast_to(v[None], (n,) + v.shape), axes, 0, 0)


def split(v, n):
    parts = []
    for _ in range(n):
        top = lax.reduce_precision(v, 8, 7)
        parts.append(top.astype(BF16))
        v = v - top
    return parts


def local(
    attention, residual, out_weight, norm_gain, lengths, adapter, images, log_scale, logit_bias
):
    zl, x, c = lax.axis_index("zl"), lax.axis_index("x"), lax.axis_index("c")
    zh, y = lax.axis_index("zh"), lax.axis_index("y")
    tok_rows = attention.shape[0]
    captions = lengths.shape[0]
    seq_len = tok_rows // captions
    half = 304

    image_norm = jnp.sqrt(jnp.sum(images * images, axis=1, keepdims=True) + 1e-06)
    picture = images / image_norm

    far_a = swap(attention[:half], "zh")
    rows = jnp.concatenate([out_weight, adapter.T, jnp.zeros((4, 512), BF16)], axis=0)
    rows = gather(rows, ("zl",))
    near = around_y(attention)
    rows, far_a, near = lax.optimization_barrier((rows, far_a, near))
    far_b = swap(attention[half:], "zh")
    far_a = around_y(far_a)
    rows = gather(rows, ("x",))
    rows, far_a, far_b = lax.optimization_barrier((rows, far_a, far_b))
    other = swap(rows, "c")
    far_b = around_y(far_b)
    pictures = gather(picture, ("zl",))
    first, second = jnp.where(c == 0, rows, other), jnp.where(c == 0, other, rows)
    both = jnp.stack([first, second], axis=2).transpose(1, 0, 2, 3, 4)
    weight = both[:, :, :, :64].reshape(2, 4, 512, 512)
    full_adapter = both[:, :, :, 64:84].reshape(1280, 512)

    near_w = lax.dynamic_index_in_dim(weight, zh, 0, keepdims=False)
    far_w = lax.dynamic_index_in_dim(weight, 1 - zh, 0, keepdims=False)
    hidden = residual.astype(F32)
    hidden = add_products(hidden, near, near_w, y)
    top = add_products(hidden[:half], far_a, far_w, y)
    low = add_products(hidden[half:], far_b, far_w, y)
    hidden = jnp.concatenate([top, low], axis=0)

    squares = jnp.sum(hidden * hidden, axis=1)
    squares, pictures = lax.optimization_barrier((squares, pictures))
    squares = jnp.sum(gather(squares, TP), axis=0)
    every_image = lax.all_gather(pictures, ("x", "c")).reshape(512, 1280)
    normed = hidden * lax.rsqrt(squares / 4096 + 1e-05)[:, None] * norm_gain[None, :]
    normed = normed.reshape(captions, seq_len, 512)
    positions = jnp.arange(seq_len, dtype=jnp.int32)
    live_mask = (positions[None, :] < lengths[:, None]).astype(F32)
    summed = jnp.sum(normed * live_mask[:, :, None], axis=1)
    pooled = (summed / lengths.astype(F32)[:, None]).astype(BF16)
    partial_text = lax.dot_general(
        pooled, full_adapter, (((1,), (1,)), ((), ())), preferred_element_type=F32
    )
    raw_text = jnp.sum(gather(partial_text, TP), axis=0)
    text_norm = jnp.sqrt(jnp.sum(raw_text * raw_text, axis=1, keepdims=True) + 1e-06)
    text_unit = raw_text / text_norm

    texts = gather(gather(text_unit.astype(F16), ("zl",)), ("x",))
    other_texts = swap(texts, "c")
    texts = texts.reshape(256, 1280).astype(F32)
    other_texts = other_texts.reshape(256, 1280).astype(F32)

    logit_scale = jnp.exp(log_scale[0])
    bias_value = logit_bias[0]
    first_row = ((x * 2 + c) * 8 + zl) * captions
    row_ids = first_row + jnp.arange(captions, dtype=jnp.int32)
    column_ids = jnp.arange(512, dtype=jnp.int32)
    labels = (column_ids[None, :] == row_ids[:, None]).astype(F32)
    logits = logit_scale * jnp.dot(text_unit, every_image.T, precision=lax.Precision.HIGHEST) + bias_value
    pair_slope = jax.nn.sigmoid(logits) - labels
    text_grad = logit_scale * jnp.dot(pair_slope, every_image, precision=lax.Precision.HIGHEST)
    raw_grad = (
        text_grad - text_unit * jnp.sum(text_unit * text_grad, axis=1, keepdims=True)
    ) / text_norm
    parts = jnp.concatenate(split(raw_grad, 3), axis=0)
    pooled_grad = jnp.dot(parts, full_adapter, preferred_element_type=F32)
    pooled_grad = jnp.sum(pooled_grad.reshape(3, captions, 512), axis=0)

    t = jnp.arange(256, dtype=jnp.int32)
    pair_of = (t // 64 * 2 + c) * 64 + t % 64
    half_labels = (column_ids[None, :] == pair_of[:, None]).astype(F32)
    half_logits = logit_scale * jnp.dot(texts, every_image.T, precision=lax.Precision.HIGH) + bias_value
    half_total = -jnp.sum(jax.nn.log_sigmoid((2.0 * half_labels - 1.0) * half_logits))
    pair_total = half_total + swap(half_total, "c")
    mean_loss = (pair_total / (512 * 512)).reshape(1)

    own_ids = (x * 8 + zl) * captions + jnp.arange(captions, dtype=jnp.int32)
    own = (t[None, :] == own_ids[:, None]).astype(F32)
    picture_grad = 0.0
    for some, mark in ((texts, own), (other_texts, 0.0)):
        slope = jnp.dot(picture, some.T, precision=lax.Precision.HIGHEST)
        slope = jax.nn.sigmoid(logit_scale * slope + bias_value) - mark
        picture_grad += jnp.dot(slope, some, precision=lax.Precision.HIGHEST)
    picture_grad = logit_scale * picture_grad
    image_grad = (
        picture_grad - picture * jnp.sum(picture * picture_grad, axis=1, keepdims=True)
    ) / image_norm
    return (mean_loss, pooled_grad, image_grad)


def solution(mesh):
    dp, tp = ("zl", "x", "c"), TP
    finer = Mesh(mesh.devices.reshape(8, 4, 2, 2, 4), dp + tp)
    placed = (P(dp, tp), P(dp, tp), P(dp, tp), P(tp), P(dp), P(tp, dp), P(dp, None), P(), P())
    return jax.shard_map(
        local,
        mesh=finer,
        in_specs=placed,
        out_specs=(P(), P(dp, tp), P(dp, None)),
        check_vma=False,
    )
```

```python
import jax
import jax.numpy as jnp
from jax import lax
from jax.sharding import Mesh, PartitionSpec as P

F32 = jnp.float32
BF16 = jnp.bfloat16
F16 = jnp.float16
SIZES = {"zl": 8, "x": 4, "c": 2, "zh": 2, "y": 4}
TP = ("zh", "y")


def swap(v, axis):
    return lax.ppermute(v, axis, [(0, 1), (1, 0)])


def shift(v, axis, by):
    n = SIZES[axis]
    return lax.ppermute(v, axis, [(i, (i + by) % n) for i in range(n)])


def around_y(v):
    return [v] + [shift(v, "y", s) for s in (1, 2, 3)]


def in_order(blocks, y):
    whole = jnp.zeros((blocks[0].shape[0], 2048), BF16)
    for back, block in enumerate(blocks):
        whole = lax.dynamic_update_slice(whole, block, (0, (y - back) % 4 * 512))
    return whole


def gather(v, axes):
    n = 1
    for a in axes:
        n *= SIZES[a]
    return lax.all_to_all(jnp.broadcast_to(v[None], (n,) + v.shape), axes, 0, 0)


def unscaled(message):
    message = message.reshape(256, 1408).astype(F32)
    return message[:, :1280] * jnp.exp2(message[:, 1280:1281])


def split(v, n):
    parts = []
    for _ in range(n):
        top = lax.reduce_precision(v, 8, 7)
        parts.append(top.astype(BF16))
        v = v - top
    return parts


def local(
    attention, residual, out_weight, norm_gain, lengths, adapter, images, log_scale, logit_bias
):
    zl, x, c = lax.axis_index("zl"), lax.axis_index("x"), lax.axis_index("c")
    zh, y = lax.axis_index("zh"), lax.axis_index("y")
    tok_rows = attention.shape[0]
    captions = lengths.shape[0]
    seq_len = tok_rows // captions
    half = 304

    image_norm = jnp.sqrt(jnp.sum(images * images, axis=1, keepdims=True) + 1e-06)
    picture = images / image_norm

    far_a = swap(attention[:half], "zh")
    rows = jnp.concatenate([out_weight, adapter.T, jnp.zeros((4, 512), BF16)], axis=0)
    rows = gather(rows, ("zl",))
    near = around_y(attention)
    rows, far_a, near = lax.optimization_barrier((rows, far_a, near))
    near = in_order(near, y)
    far_b = swap(attention[half:], "zh")
    far_a = around_y(far_a)
    rows = gather(rows, ("x",))
    rows, far_a, far_b, near = lax.optimization_barrier((rows, in_order(far_a, y), far_b, near))
    other = swap(rows, "c")
    far_b = around_y(far_b)
    other, picture = lax.optimization_barrier((other, picture))
    pictures = gather(picture, ("zl",))
    first, second = jnp.where(c == 0, rows, other), jnp.where(c == 0, other, rows)
    both = jnp.stack([first, second], axis=2).transpose(1, 0, 2, 3, 4)
    weight = both[:, :, :, :64].reshape(2, 2048, 512)
    full_adapter = both[:, :, :, 64:84].reshape(1280, 512)

    near_w = lax.dynamic_index_in_dim(weight, zh, 0, keepdims=False)
    far_w = lax.dynamic_index_in_dim(weight, 1 - zh, 0, keepdims=False)
    hidden = residual.astype(F32) + jnp.dot(near, near_w, preferred_element_type=F32)
    top = hidden[:half] + jnp.dot(far_a, far_w, preferred_element_type=F32)
    low = hidden[half:] + jnp.dot(in_order(far_b, y), far_w, preferred_element_type=F32)
    hidden = jnp.concatenate([top, low], axis=0)

    squares = jnp.sum(hidden * hidden, axis=1)
    squares, pictures = lax.optimization_barrier((squares, pictures))
    squares = jnp.sum(gather(squares, TP), axis=0)
    every_image = lax.all_gather(pictures, ("x", "c")).reshape(512, 1280)
    normed = hidden * lax.rsqrt(squares / 4096 + 1e-05)[:, None] * norm_gain[None, :]
    normed = normed.reshape(captions, seq_len, 512)
    positions = jnp.arange(seq_len, dtype=jnp.int32)
    live_mask = (positions[None, :] < lengths[:, None]).astype(F32)
    summed = jnp.sum(normed * live_mask[:, :, None], axis=1)
    pooled = (summed / lengths.astype(F32)[:, None]).astype(BF16)
    partial_text = lax.dot_general(
        pooled, full_adapter, (((1,), (1,)), ((), ())), preferred_element_type=F32
    )
    raw_text = jnp.sum(gather(partial_text, ("y",)), axis=0)
    raw_text = raw_text + swap(raw_text, "zh")
    text_norm = jnp.sqrt(jnp.sum(raw_text * raw_text, axis=1, keepdims=True) + 1e-06)
    text_unit = raw_text / text_norm

    largest = jnp.max(jnp.abs(text_unit), axis=1, keepdims=True)
    power = jnp.floor(jnp.log2(jnp.clip(largest, 1e-36, 1.0)))
    message = jnp.concatenate([text_unit * jnp.exp2(-power), jnp.broadcast_to(power, (captions, 128))], axis=1)
    texts = gather(message.astype(F16), ("zl",))
    texts, text_unit = lax.optimization_barrier((texts, text_unit))
    texts = gather(texts, ("x",))

    logit_scale = jnp.exp(log_scale[0])
    bias_value = logit_bias[0]
    first_row = ((x * 2 + c) * 8 + zl) * captions
    row_ids = first_row + jnp.arange(captions, dtype=jnp.int32)
    column_ids = jnp.arange(512, dtype=jnp.int32)
    labels = (column_ids[None, :] == row_ids[:, None]).astype(F32)
    logits = logit_scale * jnp.dot(text_unit, every_image.T, precision=lax.Precision.HIGHEST) + bias_value
    pair_slope = jax.nn.sigmoid(logits) - labels
    text_grad = logit_scale * jnp.dot(pair_slope, every_image, precision=lax.Precision.HIGHEST)
    raw_grad = (
        text_grad - text_unit * jnp.sum(text_unit * text_grad, axis=1, keepdims=True)
    ) / text_norm
    parts = jnp.concatenate(split(raw_grad, 3), axis=0)
    pooled_grad = jnp.dot(parts, full_adapter, preferred_element_type=F32)
    pooled_grad = jnp.sum(pooled_grad.reshape(3, captions, 512), axis=0)

    texts, pooled_grad = lax.optimization_barrier((texts, pooled_grad))
    other_texts = swap(texts, "c")
    texts = unscaled(texts)

    t = jnp.arange(256, dtype=jnp.int32)
    pair_of = (t // 64 * 2 + c) * 64 + t % 64
    half_labels = (column_ids[None, :] == pair_of[:, None]).astype(F32)
    half_logits = logit_scale * jnp.dot(texts, every_image.T, precision=lax.Precision.HIGH) + bias_value
    half_total = -jnp.sum(jax.nn.log_sigmoid((2.0 * half_labels - 1.0) * half_logits))
    other_texts, half_total = lax.optimization_barrier((other_texts, half_total))
    other_texts = unscaled(other_texts)
    pair_total = half_total + swap(half_total, "c")
    mean_loss = (pair_total / (512 * 512)).reshape(1)

    own_ids = (x * 8 + zl) * captions + jnp.arange(captions, dtype=jnp.int32)
    own = (t[None, :] == own_ids[:, None]).astype(F32)
    picture_grad = 0.0
    for some, mark in ((texts, own), (other_texts, 0.0)):
        slope = jnp.dot(picture, some.T, precision=lax.Precision.HIGHEST)
        slope = jax.nn.sigmoid(logit_scale * slope + bias_value) - mark
        picture_grad += jnp.dot(slope, some, precision=lax.Precision.HIGHEST)
    picture_grad = logit_scale * picture_grad
    image_grad = (
        picture_grad - picture * jnp.sum(picture * picture_grad, axis=1, keepdims=True)
    ) / image_norm
    return (mean_loss, pooled_grad, image_grad)


def solution(mesh):
    dp, tp = ("zl", "x", "c"), TP
    finer = Mesh(mesh.devices.reshape(8, 4, 2, 2, 4), dp + tp)
    placed = (P(dp, tp), P(dp, tp), P(dp, tp), P(tp), P(dp), P(tp, dp), P(dp, None), P(), P())
    return jax.shard_map(
        local,
        mesh=finer,
        in_specs=placed,
        out_specs=(P(), P(dp, tp), P(dp, None)),
        check_vma=False,
    )
```

```python
import jax
import jax.numpy as jnp
from jax import lax
from jax.sharding import Mesh, PartitionSpec as P

F32 = jnp.float32
BF16 = jnp.bfloat16
F16 = jnp.float16
SIZES = {"zl": 8, "x": 4, "c": 2, "zh": 2, "y": 4}
TP = ("zh", "y")


def swap(v, axis):
    return lax.ppermute(v, axis, [(0, 1), (1, 0)])


def shift(v, axis, by):
    n = SIZES[axis]
    return lax.ppermute(v, axis, [(i, (i + by) % n) for i in range(n)])


def around_y(v):
    return [v] + [shift(v, "y", s) for s in (1, 2, 3)]


def in_order(blocks, y):
    whole = jnp.zeros((blocks[0].shape[0], 2048), BF16)
    for back, block in enumerate(blocks):
        whole = lax.dynamic_update_slice(whole, block, (0, (y - back) % 4 * 512))
    return whole


def gather(v, axes):
    n = 1
    for a in axes:
        n *= SIZES[a]
    return lax.all_to_all(jnp.broadcast_to(v[None], (n,) + v.shape), axes, 0, 0)


def unscaled(message):
    message = message.reshape(256, 1408).astype(F32)
    return message[:, :1280] * jnp.exp2(message[:, 1280:1281])


def split(v, n):
    parts = []
    for _ in range(n):
        top = lax.reduce_precision(v, 8, 7)
        parts.append(top.astype(BF16))
        v = v - top
    return parts


def local(
    attention, residual, out_weight, norm_gain, lengths, adapter, images, log_scale, logit_bias
):
    zl, x, c = lax.axis_index("zl"), lax.axis_index("x"), lax.axis_index("c")
    zh, y = lax.axis_index("zh"), lax.axis_index("y")
    tok_rows = attention.shape[0]
    captions = lengths.shape[0]
    seq_len = tok_rows // captions
    half = 304

    image_norm = jnp.sqrt(jnp.sum(images * images, axis=1, keepdims=True) + 1e-06)
    picture = images / image_norm

    far_a = swap(attention[:half], "zh")
    rows = jnp.concatenate([out_weight, adapter.T, jnp.zeros((4, 512), BF16)], axis=0)
    rows = gather(rows, ("zl",))
    near = around_y(attention)
    rows, far_a, near = lax.optimization_barrier((rows, far_a, near))
    near = in_order(near, y)
    far_b = swap(attention[half:], "zh")
    far_a = around_y(far_a)
    rows = gather(rows, ("x",))
    rows, far_a, far_b, near = lax.optimization_barrier((rows, in_order(far_a, y), far_b, near))
    other = swap(rows, "c")
    far_b = around_y(far_b)
    pictures = gather(picture, ("zl",))
    first, second = jnp.where(c == 0, rows, other), jnp.where(c == 0, other, rows)
    both = jnp.stack([first, second], axis=2).transpose(1, 0, 2, 3, 4)
    weight = both[:, :, :, :64].reshape(2, 2048, 512)
    full_adapter = both[:, :, :, 64:84].reshape(1280, 512)

    near_w = lax.dynamic_index_in_dim(weight, zh, 0, keepdims=False)
    far_w = lax.dynamic_index_in_dim(weight, 1 - zh, 0, keepdims=False)
    hidden = residual.astype(F32) + jnp.dot(near, near_w, preferred_element_type=F32)
    top = hidden[:half] + jnp.dot(far_a, far_w, preferred_element_type=F32)
    low = hidden[half:] + jnp.dot(in_order(far_b, y), far_w, preferred_element_type=F32)
    hidden = jnp.concatenate([top, low], axis=0)

    squares = jnp.sum(hidden * hidden, axis=1)
    squares, pictures = lax.optimization_barrier((squares, pictures))
    squares = jnp.sum(gather(squares, TP), axis=0)
    every_image = lax.all_gather(pictures, ("x", "c")).reshape(512, 1280)
    normed = hidden * lax.rsqrt(squares / 4096 + 1e-05)[:, None] * norm_gain[None, :]
    normed = normed.reshape(captions, seq_len, 512)
    positions = jnp.arange(seq_len, dtype=jnp.int32)
    live_mask = (positions[None, :] < lengths[:, None]).astype(F32)
    summed = jnp.sum(normed * live_mask[:, :, None], axis=1)
    pooled = (summed / lengths.astype(F32)[:, None]).astype(BF16)
    partial_text = lax.dot_general(
        pooled, full_adapter, (((1,), (1,)), ((), ())), preferred_element_type=F32
    )
    raw_text = jnp.sum(gather(partial_text, ("y",)), axis=0)
    raw_text = raw_text + swap(raw_text, "zh")
    text_norm = jnp.sqrt(jnp.sum(raw_text * raw_text, axis=1, keepdims=True) + 1e-06)
    text_unit = raw_text / text_norm

    largest = jnp.max(jnp.abs(text_unit), axis=1, keepdims=True)
    power = jnp.floor(jnp.log2(jnp.clip(largest, 1e-36, 1.0)))
    message = jnp.concatenate([text_unit * jnp.exp2(-power), jnp.broadcast_to(power, (captions, 128))], axis=1)
    texts = gather(message.astype(F16), ("zl",))
    texts, text_unit = lax.optimization_barrier((texts, text_unit))
    texts = gather(texts, ("x",))

    logit_scale = jnp.exp(log_scale[0])
    bias_value = logit_bias[0]
    first_row = ((x * 2 + c) * 8 + zl) * captions
    row_ids = first_row + jnp.arange(captions, dtype=jnp.int32)
    column_ids = jnp.arange(512, dtype=jnp.int32)
    labels = (column_ids[None, :] == row_ids[:, None]).astype(F32)
    logits = logit_scale * jnp.dot(text_unit, every_image.T, precision=lax.Precision.HIGHEST) + bias_value
    pair_slope = jax.nn.sigmoid(logits) - labels
    text_grad = logit_scale * jnp.dot(pair_slope, every_image, precision=lax.Precision.HIGHEST)
    raw_grad = (
        text_grad - text_unit * jnp.sum(text_unit * text_grad, axis=1, keepdims=True)
    ) / text_norm
    parts = jnp.concatenate(split(raw_grad, 3), axis=0)
    pooled_grad = jnp.dot(parts, full_adapter, preferred_element_type=F32)
    pooled_grad = jnp.sum(pooled_grad.reshape(3, captions, 512), axis=0)

    texts, pooled_grad = lax.optimization_barrier((texts, pooled_grad))
    other_texts = swap(texts, "c")
    texts = unscaled(texts)

    t = jnp.arange(256, dtype=jnp.int32)
    pair_of = (t // 64 * 2 + c) * 64 + t % 64
    half_labels = (column_ids[None, :] == pair_of[:, None]).astype(F32)
    half_logits = logit_scale * jnp.dot(texts, every_image.T, precision=lax.Precision.HIGH) + bias_value
    half_total = -jnp.sum(jax.nn.log_sigmoid((2.0 * half_labels - 1.0) * half_logits))
    other_texts, half_total = lax.optimization_barrier((other_texts, half_total))
    other_texts = unscaled(other_texts)
    pair_total = half_total + swap(half_total, "c")
    mean_loss = (pair_total / (512 * 512)).reshape(1)

    own_ids = (x * 8 + zl) * captions + jnp.arange(captions, dtype=jnp.int32)
    own = (t[None, :] == own_ids[:, None]).astype(F32)
    picture_grad = 0.0
    for some, mark in ((texts, own), (other_texts, 0.0)):
        slope = jnp.dot(picture, some.T, precision=lax.Precision.HIGHEST)
        slope = jax.nn.sigmoid(logit_scale * slope + bias_value) - mark
        picture_grad += jnp.dot(slope, some, precision=lax.Precision.HIGHEST)
    picture_grad = logit_scale * picture_grad
    image_grad = (
        picture_grad - picture * jnp.sum(picture * picture_grad, axis=1, keepdims=True)
    ) / image_norm
    return (mean_loss, pooled_grad, image_grad)


def solution(mesh):
    dp, tp = ("zl", "x", "c"), TP
    finer = Mesh(mesh.devices.reshape(8, 4, 2, 2, 4), dp + tp)
    placed = (P(dp, tp), P(dp, tp), P(dp, tp), P(tp), P(dp), P(tp, dp), P(dp, None), P(), P())
    return jax.shard_map(
        local,
        mesh=finer,
        in_specs=placed,
        out_specs=(P(), P(dp, tp), P(dp, None)),
        check_vma=False,
    )
```

```python
import jax
import jax.numpy as jnp
from jax import lax
from jax.sharding import Mesh, PartitionSpec as P

F32 = jnp.float32
BF16 = jnp.bfloat16
F16 = jnp.float16
SIZES = {"zl": 8, "x": 4, "c": 2, "zh": 2, "y": 4}
TP = ("zh", "y")


def swap(v, axis):
    return lax.ppermute(v, axis, [(0, 1), (1, 0)])


def shift(v, axis, by):
    n = SIZES[axis]
    return lax.ppermute(v, axis, [(i, (i + by) % n) for i in range(n)])


def around_y(v):
    return [v] + [shift(v, "y", s) for s in (1, 2, 3)]


def in_order(blocks, y):
    whole = jnp.zeros((blocks[0].shape[0], 2048), BF16)
    for back, block in enumerate(blocks):
        whole = lax.dynamic_update_slice(whole, block, (0, (y - back) % 4 * 512))
    return whole


def gather(v, axes):
    n = 1
    for a in axes:
        n *= SIZES[a]
    return lax.all_to_all(jnp.broadcast_to(v[None], (n,) + v.shape), axes, 0, 0)


def unscaled(message):
    message = message.reshape(256, 1408).astype(F32)
    return message[:, :1280] * jnp.exp2(message[:, 1280:1281])


def split(v, n):
    parts = []
    for _ in range(n):
        top = lax.reduce_precision(v, 8, 7)
        parts.append(top.astype(BF16))
        v = v - top
    return parts


def local(
    attention, residual, out_weight, norm_gain, lengths, adapter, images, log_scale, logit_bias
):
    zl, x, c = lax.axis_index("zl"), lax.axis_index("x"), lax.axis_index("c")
    zh, y = lax.axis_index("zh"), lax.axis_index("y")
    tok_rows = attention.shape[0]
    captions = lengths.shape[0]
    seq_len = tok_rows // captions
    half = 304

    image_norm = jnp.sqrt(jnp.sum(images * images, axis=1, keepdims=True) + 1e-06)
    picture = images / image_norm

    far_a = swap(attention[:half], "zh")
    rows = gather(out_weight, ("zl",))
    near = around_y(attention)
    rows, far_a, near = lax.optimization_barrier((rows, far_a, near))
    near = in_order(near, y)
    far_b = swap(attention[half:], "zh")
    far_a = around_y(far_a)
    rows = gather(rows, ("x",))
    rows, far_a, far_b, near = lax.optimization_barrier((rows, in_order(far_a, y), far_b, near))
    other = swap(rows, "c")
    far_b = around_y(far_b)
    high, low = split(picture, 2)
    packed = [high[:, :512], high[:, 512:1024], low[:, :512], low[:, 512:1024]]
    packed += [jnp.concatenate([high[:, 1024:], low[:, 1024:]], axis=1)]
    packed = jnp.concatenate(packed + [adapter.T, jnp.zeros((4, 512), BF16)], axis=0)
    packed = gather(packed, ("zl",))
    first, second = jnp.where(c == 0, rows, other), jnp.where(c == 0, other, rows)
    both = jnp.stack([first, second], axis=2).transpose(1, 0, 2, 3, 4)
    weight = both.reshape(2, 2048, 512)

    near_w = lax.dynamic_index_in_dim(weight, zh, 0, keepdims=False)
    far_w = lax.dynamic_index_in_dim(weight, 1 - zh, 0, keepdims=False)
    hidden = residual.astype(F32) + jnp.dot(near, near_w, preferred_element_type=F32)
    top = hidden[:half] + jnp.dot(far_a, far_w, preferred_element_type=F32)
    low = hidden[half:] + jnp.dot(in_order(far_b, y), far_w, preferred_element_type=F32)
    hidden = jnp.concatenate([top, low], axis=0)

    squares = jnp.sum(hidden * hidden, axis=1)
    squares, packed = lax.optimization_barrier((squares, packed))
    full_adapter = lax.all_gather(packed[:, 40:], ("x", "c"))
    full_adapter = full_adapter[:, :, :20].transpose(1, 0, 2, 3).reshape(1280, 512)
    squares = jnp.sum(gather(squares, TP), axis=0)
    squares, packed = lax.optimization_barrier((squares, packed[:, :40]))
    packed = lax.all_gather(packed, ("x", "c"))
    parts = [packed[:, :, 8 * i : 8 * i + 8].reshape(512, 512) for i in range(5)]
    high = jnp.concatenate([parts[0], parts[1], parts[4][:, :256]], axis=1)
    low = jnp.concatenate([parts[2], parts[3], parts[4][:, 256:]], axis=1)
    every_image = high.astype(F32) + low.astype(F32)
    normed = hidden * lax.rsqrt(squares / 4096 + 1e-05)[:, None] * norm_gain[None, :]
    normed = normed.reshape(captions, seq_len, 512)
    positions = jnp.arange(seq_len, dtype=jnp.int32)
    live_mask = (positions[None, :] < lengths[:, None]).astype(F32)
    summed = jnp.sum(normed * live_mask[:, :, None], axis=1)
    pooled = (summed / lengths.astype(F32)[:, None]).astype(BF16)
    partial_text = lax.dot_general(
        pooled, full_adapter, (((1,), (1,)), ((), ())), preferred_element_type=F32
    )
    raw_text = jnp.sum(gather(partial_text, ("y",)), axis=0)
    raw_text = raw_text + swap(raw_text, "zh")
    text_norm = jnp.sqrt(jnp.sum(raw_text * raw_text, axis=1, keepdims=True) + 1e-06)
    text_unit = raw_text / text_norm

    largest = jnp.max(jnp.abs(text_unit), axis=1, keepdims=True)
    power = jnp.floor(jnp.log2(jnp.clip(largest, 1e-36, 1.0)))
    message = jnp.concatenate([text_unit * jnp.exp2(-power), jnp.broadcast_to(power, (captions, 128))], axis=1)
    texts = gather(message.astype(F16), ("zl",))
    texts, text_unit = lax.optimization_barrier((texts, text_unit))
    texts = gather(texts, ("x",))

    logit_scale = jnp.exp(log_scale[0])
    bias_value = logit_bias[0]
    first_row = ((x * 2 + c) * 8 + zl) * captions
    row_ids = first_row + jnp.arange(captions, dtype=jnp.int32)
    column_ids = jnp.arange(512, dtype=jnp.int32)
    labels = (column_ids[None, :] == row_ids[:, None]).astype(F32)
    logits = logit_scale * jnp.dot(text_unit, every_image.T, precision=lax.Precision.HIGHEST) + bias_value
    pair_slope = jax.nn.sigmoid(logits) - labels
    text_grad = logit_scale * jnp.dot(pair_slope, every_image, precision=lax.Precision.HIGHEST)
    raw_grad = (
        text_grad - text_unit * jnp.sum(text_unit * text_grad, axis=1, keepdims=True)
    ) / text_norm
    parts = jnp.concatenate(split(raw_grad, 3), axis=0)
    pooled_grad = jnp.dot(parts, full_adapter, preferred_element_type=F32)
    pooled_grad = jnp.sum(pooled_grad.reshape(3, captions, 512), axis=0)

    texts, pooled_grad = lax.optimization_barrier((texts, pooled_grad))
    other_texts = swap(texts, "c")
    texts = unscaled(texts)

    t = jnp.arange(256, dtype=jnp.int32)
    pair_of = (t // 64 * 2 + c) * 64 + t % 64
    half_labels = (column_ids[None, :] == pair_of[:, None]).astype(F32)
    half_logits = logit_scale * jnp.dot(texts, every_image.T, precision=lax.Precision.HIGH) + bias_value
    half_total = -jnp.sum(jax.nn.log_sigmoid((2.0 * half_labels - 1.0) * half_logits))
    other_texts, half_total = lax.optimization_barrier((other_texts, half_total))
    other_texts = unscaled(other_texts)
    pair_total = half_total + swap(half_total, "c")
    mean_loss = (pair_total / (512 * 512)).reshape(1)

    own_ids = (x * 8 + zl) * captions + jnp.arange(captions, dtype=jnp.int32)
    own = (t[None, :] == own_ids[:, None]).astype(F32)
    picture_grad = 0.0
    for some, mark in ((texts, own), (other_texts, 0.0)):
        slope = jnp.dot(picture, some.T, precision=lax.Precision.HIGHEST)
        slope = jax.nn.sigmoid(logit_scale * slope + bias_value) - mark
        picture_grad += jnp.dot(slope, some, precision=lax.Precision.HIGHEST)
    picture_grad = logit_scale * picture_grad
    image_grad = (
        picture_grad - picture * jnp.sum(picture * picture_grad, axis=1, keepdims=True)
    ) / image_norm
    return (mean_loss, pooled_grad, image_grad)


def solution(mesh):
    dp, tp = ("zl", "x", "c"), TP
    finer = Mesh(mesh.devices.reshape(8, 4, 2, 2, 4), dp + tp)
    placed = (P(dp, tp), P(dp, tp), P(dp, tp), P(tp), P(dp), P(tp, dp), P(dp, None), P(), P())
    return jax.shard_map(
        local,
        mesh=finer,
        in_specs=placed,
        out_specs=(P(), P(dp, tp), P(dp, None)),
        check_vma=False,
    )
```

```python
import jax
import jax.numpy as jnp
from jax import lax
from jax.sharding import Mesh, PartitionSpec as P

F32 = jnp.float32
BF16 = jnp.bfloat16
F16 = jnp.float16
SIZES = {"zl": 8, "x": 4, "c": 2, "zh": 2, "y": 4}
TP = ("zh", "y")


def swap(v, axis):
    return lax.ppermute(v, axis, [(0, 1), (1, 0)])


def shift(v, axis, by):
    n = SIZES[axis]
    return lax.ppermute(v, axis, [(i, (i + by) % n) for i in range(n)])


def around_y(v):
    return [v] + [shift(v, "y", s) for s in (1, 2, 3)]


def in_order(blocks, y):
    whole = jnp.zeros((blocks[0].shape[0], 2048), BF16)
    for back, block in enumerate(blocks):
        whole = lax.dynamic_update_slice(whole, block, (0, (y - back) % 4 * 512))
    return whole


def gather(v, axes):
    n = 1
    for a in axes:
        n *= SIZES[a]
    return lax.all_to_all(jnp.broadcast_to(v[None], (n,) + v.shape), axes, 0, 0)


def power_of(v, axis):
    largest = jnp.max(jnp.abs(v), axis=axis, keepdims=True)
    return jnp.floor(jnp.log2(jnp.clip(largest, 1e-36, 1.0)))


def unscaled(message):
    message = message.reshape(256, 1408).astype(F32)
    return message[:, :1280] * jnp.exp2(message[:, 1280:1281])


def split(v, n):
    parts = []
    for _ in range(n):
        top = lax.reduce_precision(v, 8, 7)
        parts.append(top.astype(BF16))
        v = v - top
    return parts


def local(
    attention, residual, out_weight, norm_gain, lengths, adapter, images, log_scale, logit_bias
):
    zl, x, c = lax.axis_index("zl"), lax.axis_index("x"), lax.axis_index("c")
    zh, y = lax.axis_index("zh"), lax.axis_index("y")
    tok_rows = attention.shape[0]
    captions = lengths.shape[0]
    seq_len = tok_rows // captions
    half = 304

    image_norm = jnp.sqrt(jnp.sum(images * images, axis=1, keepdims=True) + 1e-06)
    picture = images / image_norm

    far_a = swap(attention[:half], "zh")
    rows = gather(out_weight, ("zl",))
    near = around_y(attention)
    rows, far_a, near = lax.optimization_barrier((rows, far_a, near))
    near = in_order(near, y)
    far_b = swap(attention[half:], "zh")
    far_a = around_y(far_a)
    rows = gather(rows, ("x",))
    rows, far_a, far_b, near = lax.optimization_barrier((rows, in_order(far_a, y), far_b, near))
    other = swap(rows, "c")
    far_b = around_y(far_b)
    power, block_power = power_of(picture, 1), power_of(adapter.astype(F32), None)
    scaled = picture * jnp.exp2(-power)
    tail = jnp.concatenate([scaled[:, 1024:], jnp.broadcast_to(power, (captions, 256))], axis=1)
    columns = adapter.T.astype(F32) * jnp.exp2(-block_power)
    packed = [scaled[:, :512], scaled[:, 512:1024], tail, columns, jnp.broadcast_to(block_power, (4, 512))]
    packed = jnp.concatenate(packed, axis=0).astype(F16)
    packed = gather(packed, ("zl",))
    first, second = jnp.where(c == 0, rows, other), jnp.where(c == 0, other, rows)
    both = jnp.stack([first, second], axis=2).transpose(1, 0, 2, 3, 4)
    weight = both.reshape(2, 2048, 512)

    near_w = lax.dynamic_index_in_dim(weight, zh, 0, keepdims=False)
    far_w = lax.dynamic_index_in_dim(weight, 1 - zh, 0, keepdims=False)
    hidden = residual.astype(F32) + jnp.dot(near, near_w, preferred_element_type=F32)
    top = hidden[:half] + jnp.dot(far_a, far_w, preferred_element_type=F32)
    low = hidden[half:] + jnp.dot(in_order(far_b, y), far_w, preferred_element_type=F32)
    hidden = jnp.concatenate([top, low], axis=0)

    squares = jnp.sum(hidden * hidden, axis=1)
    squares, packed = lax.optimization_barrier((squares, packed))
    full_adapter = lax.all_gather(packed[:, 24:], ("x", "c"))
    full_adapter = full_adapter.astype(F32)
    full_adapter = (full_adapter[:, :, :20] * jnp.exp2(full_adapter[:, :, 20:21])).astype(BF16)
    full_adapter = full_adapter.transpose(1, 0, 2, 3).reshape(1280, 512)
    squares = jnp.sum(gather(squares, TP), axis=0)
    squares, packed = lax.optimization_barrier((squares, packed[:, :24]))
    packed = lax.all_gather(packed, ("x", "c"))
    parts = [packed[:, :, 8 * i : 8 * i + 8].reshape(512, 512).astype(F32) for i in range(3)]
    every_image = jnp.concatenate([parts[0], parts[1], parts[2][:, :256]], axis=1)
    every_image = every_image * jnp.exp2(parts[2][:, 256:257])
    normed = hidden * lax.rsqrt(squares / 4096 + 1e-05)[:, None] * norm_gain[None, :]
    normed = normed.reshape(captions, seq_len, 512)
    positions = jnp.arange(seq_len, dtype=jnp.int32)
    live_mask = (positions[None, :] < lengths[:, None]).astype(F32)
    summed = jnp.sum(normed * live_mask[:, :, None], axis=1)
    pooled = (summed / lengths.astype(F32)[:, None]).astype(BF16)
    partial_text = lax.dot_general(
        pooled, full_adapter, (((1,), (1,)), ((), ())), preferred_element_type=F32
    )
    raw_text = jnp.sum(gather(partial_text, ("y",)), axis=0)
    raw_text = raw_text + swap(raw_text, "zh")
    text_norm = jnp.sqrt(jnp.sum(raw_text * raw_text, axis=1, keepdims=True) + 1e-06)
    text_unit = raw_text / text_norm

    power = power_of(text_unit, 1)
    message = jnp.concatenate([text_unit * jnp.exp2(-power), jnp.broadcast_to(power, (captions, 128))], axis=1)
    texts = gather(message.astype(F16), ("zl",))
    texts, text_unit = lax.optimization_barrier((texts, text_unit))
    texts = gather(texts, ("x",))

    logit_scale = jnp.exp(log_scale[0])
    bias_value = logit_bias[0]
    first_row = ((x * 2 + c) * 8 + zl) * captions
    row_ids = first_row + jnp.arange(captions, dtype=jnp.int32)
    column_ids = jnp.arange(512, dtype=jnp.int32)
    labels = (column_ids[None, :] == row_ids[:, None]).astype(F32)
    logits = logit_scale * jnp.dot(text_unit, every_image.T, precision=lax.Precision.HIGHEST) + bias_value
    pair_slope = jax.nn.sigmoid(logits) - labels
    text_grad = logit_scale * jnp.dot(pair_slope, every_image, precision=lax.Precision.HIGHEST)
    raw_grad = (
        text_grad - text_unit * jnp.sum(text_unit * text_grad, axis=1, keepdims=True)
    ) / text_norm
    parts = jnp.concatenate(split(raw_grad, 3), axis=0)
    pooled_grad = jnp.dot(parts, full_adapter, preferred_element_type=F32)
    pooled_grad = jnp.sum(pooled_grad.reshape(3, captions, 512), axis=0)

    texts, pooled_grad = lax.optimization_barrier((texts, pooled_grad))
    other_texts = swap(texts, "c")
    texts = unscaled(texts)

    t = jnp.arange(256, dtype=jnp.int32)
    pair_of = (t // 64 * 2 + c) * 64 + t % 64
    half_labels = (column_ids[None, :] == pair_of[:, None]).astype(F32)
    half_logits = logit_scale * jnp.dot(texts, every_image.T, precision=lax.Precision.HIGH) + bias_value
    half_total = -jnp.sum(jax.nn.log_sigmoid((2.0 * half_labels - 1.0) * half_logits))
    other_texts, half_total = lax.optimization_barrier((other_texts, half_total))
    other_texts = unscaled(other_texts)
    pair_total = half_total + swap(half_total, "c")
    mean_loss = (pair_total / (512 * 512)).reshape(1)

    own_ids = (x * 8 + zl) * captions + jnp.arange(captions, dtype=jnp.int32)
    own = (t[None, :] == own_ids[:, None]).astype(F32)
    picture_grad = 0.0
    for some, mark in ((texts, own), (other_texts, 0.0)):
        slope = jnp.dot(picture, some.T, precision=lax.Precision.HIGHEST)
        slope = jax.nn.sigmoid(logit_scale * slope + bias_value) - mark
        picture_grad += jnp.dot(slope, some, precision=lax.Precision.HIGHEST)
    picture_grad = logit_scale * picture_grad
    image_grad = (
        picture_grad - picture * jnp.sum(picture * picture_grad, axis=1, keepdims=True)
    ) / image_norm
    return (mean_loss, pooled_grad, image_grad)


def solution(mesh):
    dp, tp = ("zl", "x", "c"), TP
    finer = Mesh(mesh.devices.reshape(8, 4, 2, 2, 4), dp + tp)
    placed = (P(dp, tp), P(dp, tp), P(dp, tp), P(tp), P(dp), P(tp, dp), P(dp, None), P(), P())
    return jax.shard_map(
        local,
        mesh=finer,
        in_specs=placed,
        out_specs=(P(), P(dp, tp), P(dp, None)),
        check_vma=False,
    )
```
